512 devices in a mesh: row: 16 (over z), col: 32 (over x, y, core).
Axes of the slice: x: 4, y: 4, z: 16, core: 2. Of those that a mesh axis runs over, the one named last changes fastest.
Arguments:
- kernel: float32 [2, 4096, 1, 8192], P(None, 'row', None, 'col'), may hold values from 0 to 2.5, as said below
Outputs:
- factored: float32 [2, 4096, 1, 8192], P(None, 'row', None, 'col')
The draws below stay inside these ranges and needn't reach their ends.
Inputs may be any that keep to these rules, and one draw needn't show every extreme that they name: kernel holds a symmetric positive definite matrix of order 8192.
All inputs are finite; a program needn't handle non-finite values.
Results may differ from the reference program's by a relative error of at most 0.0003.
Values sent between devices are 32-bit elements; how exact they have to be, the bound alone decides.
No kernel may reach another device: no remote copies, remote signals or barrier semaphores. Data moves between devices by JAX's collectives and lax.ppermute only.
A program may use at most 64 MiB of HBM per device.

```python
import jax
import jax.numpy as jnp
from jax import lax

NB = 256
KP = 4
CB = 1
RB = 2
ORDER = 8192


base_lengths = (0.4, 0.5, 0.6, 0.45, 0.55, 0.7)


def draw_kernel(key, part):
    key = jax.random.fold_in(key, 11)
    point_key, noise_key = jax.random.split(key, 2)
    points = jax.random.uniform(point_key, (ORDER, 6), jnp.float32, 0.0, 1.0)
    total = jnp.zeros((ORDER, ORDER), jnp.float32)
    for feature in range(6):
        scaled = points[:, feature] / base_lengths[feature]
        distance = scaled[:, None] - scaled[None, :]
        total = total + distance * distance
    matrix = jnp.exp(-0.5 * total)
    noise_var = jax.random.uniform(noise_key, (ORDER,), jnp.float32, 0.1, 0.2)
    row_ids = jnp.arange(ORDER, dtype=jnp.int32)[:, None]
    col_ids = jnp.arange(ORDER, dtype=jnp.int32)[None, :]
    matrix = jnp.where(row_ids == col_ids, matrix + noise_var[:, None], matrix)
    return matrix.reshape(RB, ORDER // RB, CB, ORDER // CB)


def setup_inputs(seed: int = 0) -> dict:
    seeds = jax.random.split(jax.random.key(seed), 2)
    return {
        "kernel": draw_kernel(jax.random.fold_in(seeds[1], 71), 0),
    }


def solve_rows(factor, rows):
    return jax.scipy.linalg.solve_triangular(factor, rows.T, lower=True).T

def reference(kernel):
    matrix = kernel.reshape(ORDER, ORDER)
    width = KP * NB
    left_part = matrix[:, :width]
    for panel in range(KP):
        start = panel * NB
        stop = start + NB
        factor = jnp.linalg.cholesky(left_part[start:stop, start:stop])
        lower_rows = solve_rows(factor, left_part[stop:, start:stop])
        update = jnp.dot(lower_rows, lower_rows[:width - stop].T, precision=lax.Precision.HIGHEST)
        left_part = left_part.at[stop:, stop:].add(-update)
        column = jnp.concatenate([jnp.zeros((start, NB), jnp.float32), factor, lower_rows], axis=0)
        left_part = left_part.at[:, start:stop].set(column)
    lower_left = left_part[width:]

    def row_block(inputs):
        rows, left_rows, index = inputs
        product = jnp.dot(left_rows, lower_left.T, precision=lax.Precision.HIGHEST)
        trailing = jnp.where(index >= KP, rows[:, width:] - product, 0.0)
        return jnp.concatenate([left_rows, trailing], axis=1)
    blocks = lax.map(row_block, (matrix.reshape(ORDER // NB, NB, ORDER), left_part.reshape(ORDER // NB, NB, width), jnp.arange(ORDER // NB, dtype=jnp.int32)))
    return blocks.reshape(RB, ORDER // RB, CB, ORDER // CB)
```

```python
import jax
import jax.numpy as jnp
from jax import lax
from jax.experimental import pallas as pl
from jax.experimental.pallas import tpu as pltpu
from jax.sharding import PartitionSpec as P

KP = 4
NB = 256
F32 = jnp.float32
VMEM_LIMIT = 48 * 1024 * 1024


def _dot(a, b, dims):
    return lax.dot_general(
        a, b, (dims, ((), ())), precision=lax.Precision.HIGHEST, preferred_element_type=F32
    )


def _nn(a, b):
    return _dot(a, b, ((1,), (0,)))


def _nt(a, b):
    return _dot(a, b, ((1,), (1,)))


def _tn(a, b):
    return _dot(a, b, ((0,), (0,)))


def _factor_tile(tile):
    count = tile.shape[0] // 8
    rows = [tile[8 * s : 8 * s + 8] for s in range(count)]
    lane = lax.broadcasted_iota(jnp.int32, (8, 128), 1)
    sub = lax.broadcasted_iota(jnp.int32, (8, 128), 0)

    def spread(x):
        return jnp.broadcast_to(x, (8, 128))

    upper, inverse = [], []
    for s in range(count):
        base = 8 * s
        here = (lane >= base) & (lane < base + 8)
        cols = {t: [spread(rows[t][:, base + k : base + k + 1]) for k in range(8)] for t in range(s, count)}
        rows[s] = jnp.where(here, jnp.where(lane - base == sub, 1.0, 0.0), rows[s])
        for t in range(s + 1, count):
            rows[t] = jnp.where(here, 0.0, rows[t])
        own = cols[s]
        scales, pivots, pivot_rows = [], {}, []
        for j in range(8):
            scale = 1.0 / spread(own[j][j : j + 1, :])
            ratio = jnp.where(sub > j, own[j] * scale, 0.0)
            pivot_row = spread(rows[s][j : j + 1, :])
            for k in range(j + 1, 8):
                pivots[j, k] = spread(own[k][j : j + 1, :])
                own[k] = own[k] - ratio * pivots[j, k]
            rows[s] = rows[s] - ratio * pivot_row
            scales.append(scale)
            pivot_rows.append(pivot_row)
        for t in range(s + 1, count):
            other, row = cols[t], rows[t]
            for j in range(8):
                ratio = other[j] * scales[j]
                for k in range(j + 1, 8):
                    other[k] = other[k] - ratio * pivots[j, k]
                row = row - ratio * pivot_rows[j]
            rows[t] = row
        diag, square = own[0], own[0]
        for k in range(1, 8):
            diag = jnp.where(sub == k, own[k], diag)
            square = jnp.where(lane == base + k, own[k], square)
        root = lax.rsqrt(diag)
        square = jnp.where(sub <= lane - base, square, 0.0)
        upper.append(jnp.where(lane < base, 0.0, jnp.where(here, square, rows[s])) * root)
        inverse.append(jnp.where(lane < base + 8, rows[s], 0.0) * root)
    return jnp.concatenate(upper, 0), jnp.concatenate(inverse, 0)


def _factor_block(block):
    h = NB // 2
    u11, v11 = _factor_tile(block[:h, :h])
    u12 = _nn(v11, block[:h, h:])
    u22, v22 = _factor_tile(block[h:, h:] - _tn(u12, u12))
    v21 = -_nn(v22, _tn(u12, v11))
    zero = jnp.zeros((h, h), F32)
    upper = jnp.concatenate([jnp.concatenate([u11, u12], 1), jnp.concatenate([zero, u22], 1)], 0)
    inverse = jnp.concatenate([jnp.concatenate([v11, zero], 1), jnp.concatenate([v21, v22], 1)], 0)
    return upper, inverse


UPPER = [(i, j) for i in range(KP) for j in range(i, KP)]


def _factor_kernel(pieces, upper, inverse, work):
    for slot, (i, j) in enumerate(UPPER):
        work[i, j] = pieces[:, slot].reshape(NB, NB)

    def panel(k, _):
        u, v = _factor_block(work[k, k])
        upper[k, k] = u
        inverse[k] = v

        def solve(j, _):
            upper[k, j] = _nn(inverse[k], work[k, j])
            return 0

        lax.fori_loop(k + 1, KP, solve, 0)

        def down(i, _):
            def across(j, _):
                work[i, j] = work[i, j] - _tn(upper[k, i], upper[k, j])
                return 0

            return lax.fori_loop(i, KP, across, 0)

        lax.fori_loop(k + 1, KP, down, 0)
        return 0

    lax.fori_loop(0, KP, panel, 0)


def _finish_kernel(where, kernel, left, top, upper, inverse, out, left_rows, top_cols):
    row, col = where[0], where[1]
    for k in range(KP):
        part = jnp.concatenate([left[:, k, l].reshape(NB, NB) for l in range(2)], 0)
        head = top[k]
        for j in range(k):
            part = part - _nn(left_rows[j], upper[j, k])
            head = head - _tn(upper[j, k], top_cols[j])
        left_rows[k] = _nt(part, inverse[k])
        top_cols[k] = _nn(inverse[k], head)

    @pl.when(col >= KP)
    def _():
        total = kernel[...].reshape(2 * NB, NB)
        for k in range(KP):
            total = total - _nn(left_rows[k], top_cols[k])
        total = total.reshape(2, NB, NB)
        out[0] = jnp.where(row < KP, 0.0, total[0])
        out[1] = total[1]

    @pl.when(col < KP)
    def _():
        block = left_rows[col].reshape(2, NB, NB)
        out[0] = jnp.where(row < col, 0.0, block[0])
        out[1] = block[1]

    @pl.when((row == col) & (col < KP))
    def _():
        out[0] = upper[col, col].T


def on_device(kernel):
    rows_axis, cols_axis = lax.axis_size("row"), lax.axis_size("col")
    row_index, col_index = lax.axis_index("row"), lax.axis_index("col")
    blocks = kernel.reshape(2, NB, NB)
    thin = NB // cols_axis

    top = lax.all_gather(blocks[0], "row")[:KP]

    cut = blocks.reshape(2, cols_axis, thin, NB).swapaxes(0, 1)
    scattered = lax.all_to_all(cut, "col", 0, 0)[:KP]

    corner = lax.all_to_all(
        jnp.broadcast_to(scattered[:, 0][None], (rows_axis, KP, thin, NB)), "row", 0, 0
    )[:KP]
    corner = jnp.stack([corner[i, j] for i, j in UPPER])
    pieces = lax.all_to_all(
        jnp.broadcast_to(corner[None], (cols_axis, len(UPPER), thin, NB)), "col", 0, 0
    )
    left = lax.all_to_all(
        jnp.broadcast_to(scattered[None], (cols_axis, KP, 2, thin, NB)), "col", 0, 0
    )
    vmem = pl.BlockSpec(memory_space=pltpu.VMEM)
    params = pltpu.CompilerParams(vmem_limit_bytes=VMEM_LIMIT)
    upper, inverse = pl.pallas_call(
        _factor_kernel,
        out_shape=(
            jax.ShapeDtypeStruct((KP, KP, NB, NB), F32),
            jax.ShapeDtypeStruct((KP, NB, NB), F32),
        ),
        in_specs=[vmem],
        out_specs=(vmem, vmem),
        scratch_shapes=[pltpu.VMEM((KP, KP, NB, NB), F32)],
        compiler_params=params,
        cost_estimate=pl.CostEstimate(flops=50_000_000_000, bytes_accessed=8_000_000, transcendentals=0),
        name="factor",
    )(pieces)
    place = jnp.stack([row_index, col_index]).astype(jnp.int32)
    out = pl.pallas_call(
        _finish_kernel,
        out_shape=jax.ShapeDtypeStruct((2, NB, NB), F32),
        in_specs=[pl.BlockSpec(memory_space=pltpu.SMEM)] + [vmem] * 5,
        out_specs=vmem,
        scratch_shapes=[pltpu.VMEM((KP, 2 * NB, NB), F32), pltpu.VMEM((KP, NB, NB), F32)],
        compiler_params=params,
        cost_estimate=pl.CostEstimate(flops=10_000_000_000, bytes_accessed=8_000_000, transcendentals=0),
        name="finish",
    )(place, blocks, left, top, upper, inverse)
    return out.reshape(kernel.shape)


def solution(mesh):
    spec = P(None, "row", None, "col")
    return jax.shard_map(
        on_device, mesh=mesh, in_specs=(spec,), out_specs=spec, check_vma=False
    )
```

```python
import jax
import jax.numpy as jnp
from jax import lax
from jax.experimental import pallas as pl
from jax.experimental.pallas import tpu as pltpu
from jax.sharding import PartitionSpec as P

KP = 4
GROUP = 8
NB = 256
F32 = jnp.float32
MIB = 1024 * 1024


def _dot(a, b, dims):
    return lax.dot_general(
        a, b, (dims, ((), ())), precision=lax.Precision.HIGHEST, preferred_element_type=F32
    )


def _nn(a, b):
    return _dot(a, b, ((1,), (0,)))


def _nt(a, b):
    return _dot(a, b, ((1,), (1,)))


def _tn(a, b):
    return _dot(a, b, ((0,), (0,)))


def _factor_tile(tile):
    count = tile.shape[0] // 8
    rows = [tile[8 * s : 8 * s + 8] for s in range(count)]
    lane = lax.broadcasted_iota(jnp.int32, (8, 128), 1)
    sub = lax.broadcasted_iota(jnp.int32, (8, 128), 0)

    def spread(x):
        return jnp.broadcast_to(x, (8, 128))

    def column(x, at):
        return jnp.take_along_axis(x, jnp.full((8, 128), at, jnp.int32), axis=1)

    upper, inverse = [], []
    own = [column(rows[0], k) for k in range(8)]
    for s in range(count):
        base = 8 * s
        stop = (s // GROUP + 1) * GROUP
        last = s + 1 == stop
        here = (lane >= base) & (lane < base + 8)
        ahead = [] if last else [column(rows[s], base + 8 + k) for k in range(8)]
        below = [] if last else [column(rows[s + 1], base + k) for k in range(8)]
        after = [] if last else [column(rows[s + 1], base + 8 + k) for k in range(8)]
        cols = {t: [column(rows[t], base + k) for k in range(8)] for t in range(s + 2, stop)}
        rows[s] = jnp.where(here, jnp.where(lane - base == sub, 1.0, 0.0), rows[s])
        for t in range(s + 1, stop):
            rows[t] = jnp.where(here, 0.0, rows[t])
        scales, pivots, pivot_rows = [], {}, []
        for j in range(8):
            scale = 1.0 / spread(own[j][j : j + 1, :])
            ratio = jnp.where(sub > j, own[j], 0.0) * scale
            for k in range(j + 1, 8):
                pivots[j, k] = spread(own[k][j : j + 1, :])
                own[k] = own[k] - ratio * pivots[j, k]
            pivot_row = spread(rows[s][j : j + 1, :])
            rows[s] = rows[s] - ratio * pivot_row
            scales.append(scale)
            pivot_rows.append(pivot_row)
            if not last:
                low = below[j] * scale
                for k in range(j + 1, 8):
                    below[k] = below[k] - low * pivots[j, k]
                for k in range(8):
                    pivot = spread(ahead[k][j : j + 1, :])
                    ahead[k] = ahead[k] - ratio * pivot
                    after[k] = after[k] - low * pivot
                rows[s + 1] = rows[s + 1] - low * pivot_row
        for t in range(s + 2, stop):
            other, row = cols[t], rows[t]
            for j in range(8):
                ratio = other[j] * scales[j]
                for k in range(j + 1, 8):
                    other[k] = other[k] - ratio * pivots[j, k]
                row = row - ratio * pivot_rows[j]
            rows[t] = row
        diag, square = own[0], own[0]
        for k in range(1, 8):
            diag = jnp.where(sub == k, own[k], diag)
            square = jnp.where(lane == base + k, own[k], square)
        root = lax.rsqrt(diag)
        square = jnp.where(sub <= lane - base, square, 0.0)
        upper.append(jnp.where(lane < base, 0.0, jnp.where(here, square, rows[s])) * root)
        inverse.append(jnp.where(lane < base + 8, rows[s], 0.0) * root)
        own = after
        if last and stop < count:
            low, high = 8 * (stop - GROUP), 8 * stop
            done = jnp.concatenate(upper[-GROUP:], 0)
            kept = jnp.where(lax.broadcasted_iota(jnp.int32, done.shape, 1) < high, jnp.concatenate(inverse[-GROUP:], 0), done)
            change = _tn(done, kept)
            for t in range(stop, count):
                inside = (lane >= low) & (lane < high)
                rows[t] = jnp.where(inside, 0.0, rows[t]) - change[8 * t : 8 * t + 8]
            own = [column(rows[stop], 8 * stop + k) for k in range(8)]
    return jnp.concatenate(upper, 0), jnp.concatenate(inverse, 0)


def _factor_block(block):
    h = NB // 2
    u11, v11 = _factor_tile(block[:h, :h])
    u12 = _nn(v11, block[:h, h:])
    u22, v22 = _factor_tile(block[h:, h:] - _tn(u12, u12))
    v21 = -_nn(v22, _tn(u12, v11))
    zero = jnp.zeros((h, h), F32)
    upper = jnp.concatenate([jnp.concatenate([u11, u12], 1), jnp.concatenate([zero, u22], 1)], 0)
    inverse = jnp.concatenate([jnp.concatenate([v11, zero], 1), jnp.concatenate([v21, v22], 1)], 0)
    return upper, inverse


EARLY = [(0, 0), (0, 1), (1, 1)]
LATE = [(1, 2), (2, 2), (2, 3), (3, 3), (3, 0), (0, 2), (1, 3)]


def _fetch(pairs, sems):
    copies = [pltpu.make_async_copy(x, y, sems.at[i]) for i, (x, y) in enumerate(pairs)]
    for copy in copies:
        copy.start()
    return copies


def _early_kernel(where, own, other, upper, inverse, held, work, sems):
    core = where[1]
    copies = _fetch([(own, held.at[core]), (other, held.at[1 - core])], sems)
    for copy in copies:
        copy.wait()

    def block(slot):
        return jnp.stack([held[0, :, slot], held[1, :, slot]], 1).reshape(NB, NB)

    work[...] = block(0)

    def panel(k, _):
        u, v = _factor_block(work[...])
        upper[k] = u
        inverse[k] = v

        @pl.when(k == 0)
        def _():
            u01 = _nn(inverse[0], block(1))
            upper[2] = u01
            work[...] = block(2) - _tn(u01, u01)

        return 0

    lax.fori_loop(0, 2, panel, 0)


def _late_kernel(where, own, other, upper, inverse, over, diag, inverse_out, held, u, v, work, sems):
    core = where[1]
    copies = _fetch([(own, held.at[core]), (other, held.at[1 - core]), (upper.at[2], u), (inverse, v)], sems)
    for copy in copies:
        copy.wait()

    def block(i, j):
        slot = LATE.index((i, j))
        return jnp.stack([held[0, :, slot], held[1, :, slot]], 1).reshape(NB, NB)

    u02 = _nn(v[0], block(0, 2))
    u03 = _nt(v[0], block(3, 0))
    u12 = _nn(v[1], block(1, 2) - _tn(u[...], u02))
    u13 = _nn(v[1], block(1, 3) - _tn(u[...], u03))
    over[0], over[1], over[2], over[3] = u02, u03, u12, u13
    work[0] = block(2, 2) - _tn(u02, u02) - _tn(u12, u12)
    work[1] = block(2, 3) - _tn(u02, u03) - _tn(u12, u13)
    work[2] = block(3, 3) - _tn(u03, u03) - _tn(u13, u13)

    def panel(k, _):
        top, low = _factor_block(work[0])
        diag[k] = top
        inverse_out[k] = low

        @pl.when(k == 0)
        def _():
            u23 = _nn(inverse_out[0], work[1])
            over[4] = u23
            work[0] = work[2] - _tn(u23, u23)

        return 0

    lax.fori_loop(0, 2, panel, 0)


def _finish_kernel(
    where, kernel, own, other, top, early, inv01, over, diag, inv23,
    out, left, left_rows, top_cols, e, v, o, d, w, sems,
):
    row, core, col = where[0], where[1], where[2]
    pairs = [(own, left.at[core]), (other, left.at[1 - core]), (inv01, v.at[pl.ds(0, 2)]), (early, e)]
    pairs += [(inv23, v.at[pl.ds(2, 2)]), (over, o), (top.at[pl.ds(0, KP)], top_cols), (diag, d), (kernel, w)]
    copies = _fetch(pairs, sems)
    for copy in copies[:6]:
        copy.wait()
    offs = {(0, 1): e.at[2], (2, 3): o.at[4]}
    offs.update({at: o.at[i] for i, at in enumerate([(0, 2), (0, 3), (1, 2), (1, 3)])})
    for k in range(KP):
        part = jnp.concatenate([jnp.stack([left[0, :, k, l], left[1, :, k, l]], 1).reshape(NB, NB) for l in range(2)], 0)
        for j in range(k):
            part = part - _nn(left_rows[j], offs[j, k][...])
        left_rows[k] = _nt(part, v[k])
    for copy in copies[6:]:
        copy.wait()
    for k in range(KP):
        head = top_cols[k]
        for j in range(k):
            head = head - _tn(offs[j, k][...], top_cols[j])
        top_cols[k] = _nn(v[k], head)

    @pl.when(col >= KP)
    def _():
        total = w[...].reshape(2 * NB, NB)
        for k in range(KP):
            total = total - _nn(left_rows[k], top_cols[k])
        total = total.reshape(2, NB, NB)
        out[0] = jnp.where(row < KP, 0.0, total[0])
        out[1] = total[1]

    @pl.when(col < KP)
    def _():
        block = left_rows[col].reshape(2, NB, NB)
        out[0] = jnp.where(row < col, 0.0, block[0])
        out[1] = block[1]

    for k in range(KP):

        @pl.when((row == k) & (col == k))
        def _():
            out[0] = (e if k < 2 else d)[k % 2].T


def on_device(kernel):
    rows_axis, cols_axis = lax.axis_size("row"), lax.axis_size("col")
    row_index, col_index = lax.axis_index("row"), lax.axis_index("col")
    blocks = kernel.reshape(2, NB, NB)
    thin = NB // cols_axis

    cores = [list(range(core, cols_axis, 2)) for core in range(2)]

    def spread(x, groups, count):
        whole = jnp.broadcast_to(x[None], (count, *x.shape))
        return lax.all_to_all(whole, "col", 0, 0, axis_index_groups=groups)

    def swap(x):
        return lax.ppermute(x, "col", [(c, c ^ 1) for c in range(cols_axis)])

    top = lax.all_gather(blocks[0], "row")

    scattered = lax.all_to_all(blocks.reshape(2, cols_axis, thin, NB).swapaxes(0, 1), "col", 0, 0)[:KP]
    left_own = spread(scattered, cores, cols_axis // 2)
    left_other = swap(left_own)

    first = scattered[:, 0]
    mine = jnp.stack([lax.dynamic_index_in_dim(first, lax.rem(row_index + o, KP), 0, keepdims=False) for o in range(3)])
    far = [lax.ppermute(mine, "row", [(r, r + d) for r in range(KP)]) for d in range(KP, rows_axis, KP)]
    mine = jnp.where(row_index < KP, mine, sum(far))
    mine, left_own = lax.optimization_barrier((mine, left_own))
    turned = [mine]
    for o in (1, 2, -1):
        turned.append(lax.ppermute(mine, "row", [((r + o) % rows_axis, r) for r in range(rows_axis)]))
    turned = jnp.stack(turned)
    corner = lax.dynamic_slice_in_dim(
        jnp.concatenate([turned, turned]), lax.rem(KP * rows_axis - row_index, KP), KP, 0
    )
    held = {(r, (r + o) % KP): corner[r, o] for r in range(KP) for o in range(3)}

    order = EARLY + LATE
    own = spread(jnp.stack([held[at] for at in order]), cores, cols_axis // 2)
    early_own, late_own = own[:, : len(EARLY)], own[:, len(EARLY) :]
    early_other = swap(early_own)
    late_own, _ = lax.optimization_barrier((late_own, early_other))
    late_other = swap(late_own)

    place = jnp.stack(
        [row_index, lax.rem(col_index, 2), col_index]
    ).astype(jnp.int32)
    vmem = pl.BlockSpec(memory_space=pltpu.VMEM)
    smem = pl.BlockSpec(memory_space=pltpu.SMEM)
    anywhere = pl.BlockSpec(memory_space=pl.ANY)
    params = pltpu.CompilerParams(vmem_limit_bytes=60 * MIB)

    def tiles(*lead):
        return jax.ShapeDtypeStruct((*lead, NB, NB), F32)

    def scratch(*lead):
        return pltpu.VMEM((*lead, NB, NB), F32)

    def cost(us):
        return pl.CostEstimate(flops=us * 1_000_000_000, bytes_accessed=4_000_000, transcendentals=0)

    early, inv01 = pl.pallas_call(
        _early_kernel,
        out_shape=(tiles(3), tiles(2)),
        in_specs=[smem, anywhere, anywhere],
        out_specs=(vmem, vmem),
        scratch_shapes=[
            pltpu.VMEM((2, cols_axis // 2, len(EARLY), thin, NB), F32),
            scratch(),
            pltpu.SemaphoreType.DMA((2,)),
        ],
        compiler_params=params,
        cost_estimate=cost(20),
        name="early",
    )(place, early_own, early_other)
    over, diag, inv23 = pl.pallas_call(
        _late_kernel,
        out_shape=(tiles(5), tiles(2), tiles(2)),
        in_specs=[smem] + [anywhere] * 4,
        out_specs=(vmem, vmem, vmem),
        scratch_shapes=[
            pltpu.VMEM((2, cols_axis // 2, len(LATE), thin, NB), F32),
            scratch(),
            scratch(2),
            scratch(3),
            pltpu.SemaphoreType.DMA((4,)),
        ],
        compiler_params=params,
        cost_estimate=cost(24),
        name="late",
    )(place, late_own, late_other, early, inv01)
    out = pl.pallas_call(
        _finish_kernel,
        out_shape=tiles(2),
        in_specs=[smem] + [anywhere] * 9,
        out_specs=vmem,
        scratch_shapes=[
            pltpu.VMEM((2, cols_axis // 2, KP, 2, thin, NB), F32),
            pltpu.VMEM((KP, 2 * NB, NB), F32),
            scratch(KP),
            scratch(3),
            scratch(KP),
            scratch(5),
            scratch(2),
            scratch(2),
            pltpu.SemaphoreType.DMA((9,)),
        ],
        compiler_params=params,
        cost_estimate=cost(10),
        name="finish",
    )(place, blocks, left_own, left_other, top, early, inv01, over, diag, inv23)
    return out.reshape(kernel.shape)


def solution(mesh):
    spec = P(None, "row", None, "col")
    return jax.shard_map(
        on_device, mesh=mesh, in_specs=(spec,), out_specs=spec, check_vma=False
    )
```

```python
import jax
import jax.numpy as jnp
from jax import lax
from jax.experimental import pallas as pl
from jax.experimental.pallas import tpu as pltpu
from jax.sharding import PartitionSpec as P

KP = 4
GROUP = 8
NB = 256
F32 = jnp.float32
MIB = 1024 * 1024


def _dot(a, b, dims):
    return lax.dot_general(
        a, b, (dims, ((), ())), precision=lax.Precision.HIGHEST, preferred_element_type=F32
    )


def _nn(a, b):
    return _dot(a, b, ((1,), (0,)))


def _nt(a, b):
    return _dot(a, b, ((1,), (1,)))


def _tn(a, b):
    return _dot(a, b, ((0,), (0,)))


def _factor_tile(tile):
    count = tile.shape[0] // 8
    rows = [tile[8 * s : 8 * s + 8] for s in range(count)]
    lane = lax.broadcasted_iota(jnp.int32, (8, 128), 1)
    sub = lax.broadcasted_iota(jnp.int32, (8, 128), 0)

    def spread(x):
        return jnp.broadcast_to(x, (8, 128))

    def column(x, at):
        return jnp.take_along_axis(x, jnp.full((8, 128), at, jnp.int32), axis=1)

    upper, inverse = [], []
    own = [column(rows[0], k) for k in range(8)]
    for s in range(count):
        base = 8 * s
        stop = (s // GROUP + 1) * GROUP
        last = s + 1 == stop
        here = (lane >= base) & (lane < base + 8)
        ahead = [] if last else [column(rows[s], base + 8 + k) for k in range(8)]
        below = [] if last else [column(rows[s + 1], base + k) for k in range(8)]
        after = [] if last else [column(rows[s + 1], base + 8 + k) for k in range(8)]
        cols = {t: [column(rows[t], base + k) for k in range(8)] for t in range(s + 2, stop)}
        rows[s] = jnp.where(here, jnp.where(lane - base == sub, 1.0, 0.0), rows[s])
        for t in range(s + 1, stop):
            rows[t] = jnp.where(here, 0.0, rows[t])
        scales, pivots, pivot_rows = [], {}, []
        for j in range(8):
            scale = 1.0 / spread(own[j][j : j + 1, :])
            ratio = jnp.where(sub > j, own[j], 0.0) * scale
            for k in range(j + 1, 8):
                pivots[j, k] = spread(own[k][j : j + 1, :])
                own[k] = own[k] - ratio * pivots[j, k]
            pivot_row = spread(rows[s][j : j + 1, :])
            rows[s] = rows[s] - ratio * pivot_row
            scales.append(scale)
            pivot_rows.append(pivot_row)
            if not last:
                low = below[j] * scale
                for k in range(j + 1, 8):
                    below[k] = below[k] - low * pivots[j, k]
                for k in range(8):
                    pivot = spread(ahead[k][j : j + 1, :])
                    ahead[k] = ahead[k] - ratio * pivot
                    after[k] = after[k] - low * pivot
                rows[s + 1] = rows[s + 1] - low * pivot_row
        for t in range(s + 2, stop):
            other, row = cols[t], rows[t]
            for j in range(8):
                ratio = other[j] * scales[j]
                for k in range(j + 1, 8):
                    other[k] = other[k] - ratio * pivots[j, k]
                row = row - ratio * pivot_rows[j]
            rows[t] = row
        diag, square = own[0], own[0]
        for k in range(1, 8):
            diag = jnp.where(sub == k, own[k], diag)
            square = jnp.where(lane == base + k, own[k], square)
        root = lax.rsqrt(diag)
        square = jnp.where(sub <= lane - base, square, 0.0)
        upper.append(jnp.where(lane < base, 0.0, jnp.where(here, square, rows[s])) * root)
        inverse.append(jnp.where(lane < base + 8, rows[s], 0.0) * root)
        own = after
        if last and stop < count:
            low, high = 8 * (stop - GROUP), 8 * stop
            done = jnp.concatenate(upper[-GROUP:], 0)
            kept = jnp.where(lax.broadcasted_iota(jnp.int32, done.shape, 1) < high, jnp.concatenate(inverse[-GROUP:], 0), done)
            change = _tn(done, kept)
            for t in range(stop, count):
                inside = (lane >= low) & (lane < high)
                rows[t] = jnp.where(inside, 0.0, rows[t]) - change[8 * t : 8 * t + 8]
            own = [column(rows[stop], 8 * stop + k) for k in range(8)]
    return jnp.concatenate(upper, 0), jnp.concatenate(inverse, 0)


def _factor_block(block):
    h = NB // 2
    u11, v11 = _factor_tile(block[:h, :h])
    u12 = _nn(v11, block[:h, h:])
    u22, v22 = _factor_tile(block[h:, h:] - _tn(u12, u12))
    v21 = -_nn(v22, _tn(u12, v11))
    zero = jnp.zeros((h, h), F32)
    upper = jnp.concatenate([jnp.concatenate([u11, u12], 1), jnp.concatenate([zero, u22], 1)], 0)
    inverse = jnp.concatenate([jnp.concatenate([v11, zero], 1), jnp.concatenate([v21, v22], 1)], 0)
    return upper, inverse


EARLY = [(0, 0), (0, 1), (1, 1)]
LATE = [(1, 2), (2, 2), (2, 3), (3, 3), (3, 0), (0, 2), (1, 3)]


HALF = NB // 2


def _fetch(pairs, sems):
    copies = [pltpu.make_async_copy(x, y, sems.at[i]) for i, (x, y) in enumerate(pairs)]
    for copy in copies:
        copy.start()
    return copies


def _columns(half, rows):
    return pl.ds(half, rows, stride=2)


def _square(load):
    return jnp.concatenate([load(half).reshape(NB, HALF) for half in range(2)], 1)


def _paired(held, slot):
    def load(half):
        thin = held.shape[3] // 2
        return jnp.stack([held[core, :, slot, _columns(half, thin), :] for core in range(2)], 1)

    return _square(load)


def _early_kernel(own, other, upper, inverse, held, work, sems):
    core = lax.rem(lax.axis_index("col"), 2)
    count = len(EARLY)
    copies = _fetch([(own.at[:, pl.ds(0, count)], held.at[core]), (other, held.at[1 - core])], sems)
    for copy in copies:
        copy.wait()
    work[...] = _paired(held, 0)

    def panel(k, _):
        u, v = _factor_block(work[...])
        upper[k] = u
        inverse[k] = v

        @pl.when(k == 0)
        def _():
            u01 = _nn(inverse[0], _paired(held, 1))
            upper[2] = u01
            work[...] = _paired(held, 2) - _tn(u01, u01)

        return 0

    lax.fori_loop(0, 2, panel, 0)


def _late_kernel(own, other, upper, inverse, over, diag, inverse_out, held, u, v, sems):
    core = lax.rem(lax.axis_index("col"), 2)
    mine = own.at[:, pl.ds(len(EARLY), len(LATE))]
    copies = _fetch([(mine, held.at[core]), (other, held.at[1 - core]), (upper.at[2], u), (inverse, v)], sems)
    for copy in copies:
        copy.wait()

    def block(i, j):
        return _paired(held, LATE.index((i, j)))

    u02 = _nn(v[0], block(0, 2))
    u03 = _nt(v[0], block(3, 0))
    u12 = _nn(v[1], block(1, 2) - _tn(u[...], u02))
    u13 = _nn(v[1], block(1, 3) - _tn(u[...], u03))
    over[0], over[1], over[2], over[3] = u02, u03, u12, u13
    top, low = _factor_block(block(2, 2) - _tn(u02, u02) - _tn(u12, u12))
    u23 = _nn(low, block(2, 3) - _tn(u02, u03) - _tn(u12, u13))
    last = block(3, 3) - _tn(u03, u03) - _tn(u13, u13)
    diag[0], inverse_out[0], over[4] = top, low, u23
    diag[1], inverse_out[1] = _factor_block(last - _tn(u23, u23))


def _finish_kernel(
    kernel, left, top, early, inv01, over, diag, inv23,
    out, raw_left, raw_top, left_rows, top_cols, e, v, o, d, w, sems,
):
    row, col = lax.axis_index("row"), lax.axis_index("col")
    pairs = [(inv01, v.at[pl.ds(0, 2)]), (top.at[pl.ds(0, KP)], raw_top), (left, raw_left), (early, e), (over, o)]
    pairs += [(inv23, v.at[pl.ds(2, 2)]), (diag, d), (kernel, w)]
    copies = _fetch(pairs, sems)
    offs = {(0, 1): e.at[2], (2, 3): o.at[4]}
    offs.update({at: o.at[i] for i, at in enumerate([(0, 2), (0, 3), (1, 2), (1, 3)])})
    thin = raw_left.shape[3] // 2
    for copy in copies:
        copy.wait()
    for k in range(KP):
        head = _square(lambda half: raw_top[k, _columns(half, NB), :])
        parts = [_square(lambda half: raw_left[:, k, l, _columns(half, thin), :]) for l in range(2)]
        for j in range(k):
            head = head - _tn(offs[j, k][...], top_cols[j])
            parts = [parts[l] - _nn(left_rows[j, pl.ds(NB * l, NB)], offs[j, k][...]) for l in range(2)]
        top_cols[k] = _nn(v[k], head)
        for l in range(2):
            left_rows[k, pl.ds(NB * l, NB)] = _nt(parts[l], v[k])

    def store(l, block):
        for half in range(2):
            out[l, _columns(half, NB), :] = block[:, half * HALF : (half + 1) * HALF]

    @pl.when(col >= KP)
    def _():
        total = jnp.concatenate([_square(lambda half: w[l, _columns(half, NB), :]) for l in range(2)], 0)
        for k in range(KP):
            total = total - _nn(left_rows[k], top_cols[k])
        store(0, jnp.where(row < KP, 0.0, total[:NB]))
        store(1, total[NB:])

    @pl.when(col < KP)
    def _():
        block = left_rows[col]
        store(0, jnp.where(row < col, 0.0, block[:NB]))
        store(1, block[NB:])

    for k in range(KP):

        @pl.when((row == k) & (col == k))
        def _():
            store(0, (e if k < 2 else d)[k % 2].T)


VMEM = pl.BlockSpec(memory_space=pltpu.VMEM)
ANYWHERE = pl.BlockSpec(memory_space=pl.ANY)


def _tiles(*lead):
    return jax.ShapeDtypeStruct((*lead, NB, NB), F32)


def _scratch(*lead):
    return pltpu.VMEM((*lead, NB, NB), F32)


def _call(kernel, name, cost, copies, scratch, out_shape, operands):
    return pl.pallas_call(
        kernel,
        out_shape=out_shape,
        in_specs=[ANYWHERE] * len(operands),
        out_specs=jax.tree.map(lambda _: VMEM, out_shape),
        scratch_shapes=[*scratch, pltpu.SemaphoreType.DMA((copies,))],
        compiler_params=pltpu.CompilerParams(vmem_limit_bytes=60 * MIB),
        cost_estimate=pl.CostEstimate(flops=cost * 10**9, bytes_accessed=4_000_000, transcendentals=0),
        name=name,
    )(*operands)


def _early(own, other):
    held = pltpu.VMEM((2, *other.shape), F32)
    return _call(_early_kernel, "early", 12, 2, [held, _scratch()], (_tiles(3), _tiles(2)), (own, other))


def _late(own, other, upper, inverse):
    held = pltpu.VMEM((2, *other.shape), F32)
    return _call(
        _late_kernel,
        "late",
        16,
        4,
        [held, _scratch(), _scratch(2)],
        (_tiles(5), _tiles(2), _tiles(2)),
        (own, other, upper, inverse),
    )


def _finish(blocks, left, top, early, inv01, over, diag, inv23):
    scratch = [
        pltpu.VMEM(left.shape, F32),
        pltpu.VMEM((KP, *top.shape[1:]), F32),
        pltpu.VMEM((KP, 2 * NB, NB), F32),
        _scratch(KP),
        _scratch(3),
        _scratch(KP),
        _scratch(5),
        _scratch(2),
        pltpu.VMEM(blocks.shape, F32),
    ]
    return _call(
        _finish_kernel,
        "finish",
        10,
        8,
        scratch,
        jax.ShapeDtypeStruct(blocks.shape, F32),
        (blocks, left, top, early, inv01, over, diag, inv23),
    )


def on_device(kernel):
    rows_axis, cols_axis = lax.axis_size("row"), lax.axis_size("col")
    row_index, col_index = lax.axis_index("row"), lax.axis_index("col")
    blocks = kernel.reshape(2, 2 * NB, HALF)
    piece = (2 * NB // cols_axis, HALF)
    cores = [list(range(core, cols_axis, 2)) for core in range(2)]
    quads = [list(range(r, r + KP)) for r in range(0, rows_axis, KP)]

    def copies(x, count):
        return jnp.broadcast_to(x[None], (count, *x.shape))

    def spread(whole, axis, groups=None):
        return lax.all_to_all(whole, axis, 0, 0, axis_index_groups=groups)

    def swap(x):
        return lax.ppermute(x, "col", [(c, c ^ 1) for c in range(cols_axis)])

    cut = blocks.reshape(2, cols_axis, *piece).swapaxes(0, 1)
    scattered = lax.all_to_all(cut, "col", 0, 0)[:KP]

    lead, scattered = lax.optimization_barrier((blocks[0], scattered))
    top = lax.all_gather(lead, "row")

    first = scattered[:, 0]
    mine = jnp.stack([lax.dynamic_index_in_dim(first, lax.rem(row_index + o, KP), 0, keepdims=False) for o in range(3)])
    far = [lax.ppermute(mine, "row", [(r, r + d) for r in range(KP)]) for d in range(KP, rows_axis, KP)]
    mine = jnp.where(row_index < KP, mine, sum(far))
    mine, left = lax.optimization_barrier((mine, copies(scattered, cols_axis)))
    corner = spread(copies(mine, KP), "row", quads)

    order = [corner[r, (c - r) % KP] for r, c in EARLY + LATE]
    own = spread(copies(jnp.stack(order), cols_axis // 2), "col", cores)
    early_other = swap(own[:, : len(EARLY)])
    late_other = swap(own[:, len(EARLY) :])
    left, _ = lax.optimization_barrier((left, early_other))
    left = spread(left, "col")

    early, inv01 = _early(own, early_other)
    over, diag, inv23 = _late(own, late_other, early, inv01)
    out = _finish(blocks, left, top, early, inv01, over, diag, inv23)
    return out.reshape(kernel.shape)


def solution(mesh):
    spec = P(None, "row", None, "col")
    return jax.shard_map(
        on_device, mesh=mesh, in_specs=(spec,), out_specs=spec, check_vma=False
    )
```

```python
import jax
import jax.numpy as jnp
from jax import lax
from jax.experimental import pallas as pl
from jax.experimental.pallas import tpu as pltpu
from jax.sharding import PartitionSpec as P

KP = 4
GROUP = 8
NB = 256
F32 = jnp.float32
MIB = 1024 * 1024


def _dot(a, b, dims):
    return lax.dot_general(
        a, b, (dims, ((), ())), precision=lax.Precision.HIGHEST, preferred_element_type=F32
    )


def _nn(a, b):
    return _dot(a, b, ((1,), (0,)))


def _nt(a, b):
    return _dot(a, b, ((1,), (1,)))


def _tn(a, b):
    return _dot(a, b, ((0,), (0,)))


def _factor_tile(tile):
    count = tile.shape[0] // 8
    rows = [tile[8 * s : 8 * s + 8] for s in range(count)]
    lane = lax.broadcasted_iota(jnp.int32, (8, 128), 1)
    sub = lax.broadcasted_iota(jnp.int32, (8, 128), 0)

    def spread(x):
        return jnp.broadcast_to(x, (8, 128))

    def column(x, at):
        return jnp.take_along_axis(x, jnp.full((8, 128), at, jnp.int32), axis=1)

    upper, inverse = [], []
    own = [column(rows[0], k) for k in range(8)]
    for s in range(count):
        base = 8 * s
        stop = (s // GROUP + 1) * GROUP
        last = s + 1 == stop
        here = (lane >= base) & (lane < base + 8)
        ahead = [] if last else [column(rows[s], base + 8 + k) for k in range(8)]
        below = [] if last else [column(rows[s + 1], base + k) for k in range(8)]
        after = [] if last else [column(rows[s + 1], base + 8 + k) for k in range(8)]
        cols = {t: [column(rows[t], base + k) for k in range(8)] for t in range(s + 2, stop)}
        rows[s] = jnp.where(here, jnp.where(lane - base == sub, 1.0, 0.0), rows[s])
        for t in range(s + 1, stop):
            rows[t] = jnp.where(here, 0.0, rows[t])
        scales, pivots, pivot_rows = [], {}, []
        for j in range(8):
            scale = 1.0 / spread(own[j][j : j + 1, :])
            ratio = jnp.where(sub > j, own[j], 0.0) * scale
            for k in range(j + 1, 8):
                pivots[j, k] = spread(own[k][j : j + 1, :])
                own[k] = own[k] - ratio * pivots[j, k]
            pivot_row = spread(rows[s][j : j + 1, :])
            rows[s] = rows[s] - ratio * pivot_row
            scales.append(scale)
            pivot_rows.append(pivot_row)
            if not last:
                low = below[j] * scale
                for k in range(j + 1, 8):
                    below[k] = below[k] - low * pivots[j, k]
                for k in range(8):
                    pivot = spread(ahead[k][j : j + 1, :])
                    ahead[k] = ahead[k] - ratio * pivot
                    after[k] = after[k] - low * pivot
                rows[s + 1] = rows[s + 1] - low * pivot_row
        for t in range(s + 2, stop):
            other, row = cols[t], rows[t]
            for j in range(8):
                ratio = other[j] * scales[j]
                for k in range(j + 1, 8):
                    other[k] = other[k] - ratio * pivots[j, k]
                row = row - ratio * pivot_rows[j]
            rows[t] = row
        diag, square = own[0], own[0]
        for k in range(1, 8):
            diag = jnp.where(sub == k, own[k], diag)
            square = jnp.where(lane == base + k, own[k], square)
        root = lax.rsqrt(diag)
        square = jnp.where(sub <= lane - base, square, 0.0)
        upper.append(jnp.where(lane < base, 0.0, jnp.where(here, square, rows[s])) * root)
        inverse.append(jnp.where(lane < base + 8, rows[s], 0.0) * root)
        own = after
        if last and stop < count:
            low, high = 8 * (stop - GROUP), 8 * stop
            done = jnp.concatenate(upper[-GROUP:], 0)
            kept = jnp.where(lax.broadcasted_iota(jnp.int32, done.shape, 1) < high, jnp.concatenate(inverse[-GROUP:], 0), done)
            change = _tn(done, kept)
            for t in range(stop, count):
                inside = (lane >= low) & (lane < high)
                rows[t] = jnp.where(inside, 0.0, rows[t]) - change[8 * t : 8 * t + 8]
            own = [column(rows[stop], 8 * stop + k) for k in range(8)]
    return jnp.concatenate(upper, 0), jnp.concatenate(inverse, 0)


def _factor_block(block):
    h = NB // 2
    u11, v11 = _factor_tile(block[:h, :h])
    u12 = _nn(v11, block[:h, h:])
    u22, v22 = _factor_tile(block[h:, h:] - _tn(u12, u12))
    v21 = -_nn(v22, _tn(u12, v11))
    zero = jnp.zeros((h, h), F32)
    upper = jnp.concatenate([jnp.concatenate([u11, u12], 1), jnp.concatenate([zero, u22], 1)], 0)
    inverse = jnp.concatenate([jnp.concatenate([v11, zero], 1), jnp.concatenate([v21, v22], 1)], 0)
    return upper, inverse


EARLY = [(0, 0), (0, 1), (1, 1)]
LATE = [(1, 2), (2, 2), (2, 3), (3, 3), (3, 0), (0, 2), (1, 3)]


HALF = NB // 2


def _fetch(pairs, sems):
    copies = [pltpu.make_async_copy(x, y, sems.at[i]) for i, (x, y) in enumerate(pairs)]
    for copy in copies:
        copy.start()
    return copies


def _columns(half, rows):
    return pl.ds(half, rows, stride=2)


def _square(load):
    return jnp.concatenate([load(half).reshape(NB, HALF) for half in range(2)], 1)


def _paired(held, slot):
    def load(half):
        thin = held.shape[3] // 2
        return jnp.stack([held[core, :, slot, _columns(half, thin), :] for core in range(2)], 1)

    return _square(load)


def _early_kernel(own, other, upper, inverse, held, work, sems):
    core = lax.rem(lax.axis_index("col"), 2)
    count = len(EARLY)
    copies = _fetch([(x.at[:, pl.ds(0, count)], held.at[at]) for x, at in ((own, core), (other, 1 - core))], sems)
    for copy in copies:
        copy.wait()
    work[...] = _paired(held, 0)

    def panel(k, _):
        u, v = _factor_block(work[...])
        upper[k] = u
        inverse[k] = v

        @pl.when(k == 0)
        def _():
            u01 = _nn(inverse[0], _paired(held, 1))
            upper[2] = u01
            work[...] = _paired(held, 2) - _tn(u01, u01)

        return 0

    lax.fori_loop(0, 2, panel, 0)


def _late_kernel(own, other, upper, inverse, over, diag, inverse_out, held, u, v, sems):
    core = lax.rem(lax.axis_index("col"), 2)
    pairs = [(x.at[:, pl.ds(len(EARLY), len(LATE))], held.at[at]) for x, at in ((own, core), (other, 1 - core))]
    copies = _fetch([*pairs, (upper.at[2], u), (inverse, v)], sems)
    for copy in copies:
        copy.wait()

    def block(i, j):
        return _paired(held, LATE.index((i, j)))

    u02 = _nn(v[0], block(0, 2))
    u03 = _nt(v[0], block(3, 0))
    u12 = _nn(v[1], block(1, 2) - _tn(u[...], u02))
    u13 = _nn(v[1], block(1, 3) - _tn(u[...], u03))
    over[0], over[1], over[2], over[3] = u02, u03, u12, u13
    top, low = _factor_block(block(2, 2) - _tn(u02, u02) - _tn(u12, u12))
    u23 = _nn(low, block(2, 3) - _tn(u02, u03) - _tn(u12, u13))
    last = block(3, 3) - _tn(u03, u03) - _tn(u13, u13)
    diag[0], inverse_out[0], over[4] = top, low, u23
    diag[1], inverse_out[1] = _factor_block(last - _tn(u23, u23))


def _finish_kernel(
    kernel, left, top, early, inv01, over, diag, inv23,
    out, raw_left, raw_top, left_rows, top_cols, e, v, o, d, w, sems,
):
    row, col = lax.axis_index("row"), lax.axis_index("col")
    pairs = [(inv01, v.at[pl.ds(0, 2)]), (top.at[pl.ds(0, KP)], raw_top), (left, raw_left), (early, e), (over, o)]
    pairs += [(inv23, v.at[pl.ds(2, 2)]), (diag, d), (kernel, w)]
    copies = _fetch(pairs, sems)
    offs = {(0, 1): e.at[2], (2, 3): o.at[4]}
    offs.update({at: o.at[i] for i, at in enumerate([(0, 2), (0, 3), (1, 2), (1, 3)])})
    thin = raw_left.shape[3] // 2
    for copy in copies:
        copy.wait()
    for k in range(KP):
        head = _square(lambda half: raw_top[k, _columns(half, NB), :])
        parts = [_square(lambda half: raw_left[:, k, l, _columns(half, thin), :]) for l in range(2)]
        for j in range(k):
            head = head - _tn(offs[j, k][...], top_cols[j])
            parts = [parts[l] - _nn(left_rows[j, pl.ds(NB * l, NB)], offs[j, k][...]) for l in range(2)]
        top_cols[k] = _nn(v[k], head)
        for l in range(2):
            left_rows[k, pl.ds(NB * l, NB)] = _nt(parts[l], v[k])

    def store(l, block):
        for half in range(2):
            out[l, _columns(half, NB), :] = block[:, half * HALF : (half + 1) * HALF]

    @pl.when(col >= KP)
    def _():
        total = jnp.concatenate([_square(lambda half: w[l, _columns(half, NB), :]) for l in range(2)], 0)
        for k in range(KP):
            total = total - _nn(left_rows[k], top_cols[k])
        store(0, jnp.where(row < KP, 0.0, total[:NB]))
        store(1, total[NB:])

    @pl.when(col < KP)
    def _():
        block = left_rows[col]
        store(0, jnp.where(row < col, 0.0, block[:NB]))
        store(1, block[NB:])

    for k in range(KP):

        @pl.when((row == k) & (col == k))
        def _():
            store(0, (e if k < 2 else d)[k % 2].T)


VMEM = pl.BlockSpec(memory_space=pltpu.VMEM)
ANYWHERE = pl.BlockSpec(memory_space=pl.ANY)


def _tiles(*lead):
    return jax.ShapeDtypeStruct((*lead, NB, NB), F32)


def _scratch(*lead):
    return pltpu.VMEM((*lead, NB, NB), F32)


def _call(kernel, name, cost, copies, scratch, out_shape, operands):
    return pl.pallas_call(
        kernel,
        out_shape=out_shape,
        in_specs=[ANYWHERE] * len(operands),
        out_specs=jax.tree.map(lambda _: VMEM, out_shape),
        scratch_shapes=[*scratch, pltpu.SemaphoreType.DMA((copies,))],
        compiler_params=pltpu.CompilerParams(vmem_limit_bytes=60 * MIB),
        cost_estimate=pl.CostEstimate(flops=cost * 10**9, bytes_accessed=4_000_000, transcendentals=0),
        name=name,
    )(*operands)


def _early(own, other):
    held = pltpu.VMEM((2, own.shape[0], len(EARLY), *own.shape[2:]), F32)
    return _call(_early_kernel, "early", 12, 2, [held, _scratch()], (_tiles(3), _tiles(2)), (own, other))


def _late(own, other, upper, inverse):
    held = pltpu.VMEM((2, own.shape[0], len(LATE), *own.shape[2:]), F32)
    return _call(
        _late_kernel,
        "late",
        16,
        4,
        [held, _scratch(), _scratch(2)],
        (_tiles(5), _tiles(2), _tiles(2)),
        (own, other, upper, inverse),
    )


def _finish(blocks, left, top, early, inv01, over, diag, inv23):
    scratch = [
        pltpu.VMEM(left.shape, F32),
        pltpu.VMEM((KP, *top.shape[1:]), F32),
        pltpu.VMEM((KP, 2 * NB, NB), F32),
        _scratch(KP),
        _scratch(3),
        _scratch(KP),
        _scratch(5),
        _scratch(2),
        pltpu.VMEM(blocks.shape, F32),
    ]
    return _call(
        _finish_kernel,
        "finish",
        10,
        8,
        scratch,
        jax.ShapeDtypeStruct(blocks.shape, F32),
        (blocks, left, top, early, inv01, over, diag, inv23),
    )


def on_device(kernel):
    rows_axis, cols_axis = lax.axis_size("row"), lax.axis_size("col")
    row_index, col_index = lax.axis_index("row"), lax.axis_index("col")
    blocks = kernel.reshape(2, 2 * NB, HALF)
    piece = (2 * NB // cols_axis, HALF)
    cores = [list(range(core, cols_axis, 2)) for core in range(2)]
    quads = [list(range(r, r + KP)) for r in range(0, rows_axis, KP)]

    def copies(x, count):
        return jnp.broadcast_to(x[None], (count, *x.shape))

    def spread(whole, axis, groups=None):
        return lax.all_to_all(whole, axis, 0, 0, axis_index_groups=groups)

    def swap(x):
        return lax.ppermute(x, "col", [(c, c ^ 1) for c in range(cols_axis)])

    cut = blocks.reshape(2, cols_axis, *piece).swapaxes(0, 1)
    scattered = lax.all_to_all(cut, "col", 0, 0)[:KP]

    lead, scattered = lax.optimization_barrier((blocks[0], scattered))
    top = lax.all_gather(lead, "row")

    first = scattered[:, 0]
    mine = jnp.stack([lax.dynamic_index_in_dim(first, lax.rem(row_index + o, KP), 0, keepdims=False) for o in range(3)])
    far = [lax.ppermute(mine, "row", [(r, r + d) for r in range(KP)]) for d in range(KP, rows_axis, KP)]
    mine = jnp.where(row_index < KP, mine, sum(far))
    mine, left = lax.optimization_barrier((mine, copies(scattered, cols_axis)))
    corner = spread(copies(mine, KP), "row", quads)

    order = [corner[r, (c - r) % KP] for r, c in EARLY + LATE]
    own = spread(copies(jnp.stack(order), cols_axis // 2), "col", cores)
    other = swap(own)
    left, _ = lax.optimization_barrier((left, own))
    left = spread(left, "col")

    early, inv01 = _early(own, other)
    over, diag, inv23 = _late(own, other, early, inv01)
    out = _finish(blocks, left, top, early, inv01, over, diag, inv23)
    return out.reshape(kernel.shape)


def solution(mesh):
    spec = P(None, "row", None, "col")
    return jax.shard_map(
        on_device, mesh=mesh, in_specs=(spec,), out_specs=spec, check_vma=False
    )
```

```python
import jax
import jax.numpy as jnp
from jax import lax
from jax.experimental import pallas as pl
from jax.experimental.pallas import tpu as pltpu
from jax.sharding import PartitionSpec as P

KP = 4
GROUP = 8
NB = 256
F32 = jnp.float32
MIB = 1024 * 1024


def _dot(a, b, dims):
    return lax.dot_general(
        a, b, (dims, ((), ())), precision=lax.Precision.HIGHEST, preferred_element_type=F32
    )


def _nn(a, b):
    return _dot(a, b, ((1,), (0,)))


def _nt(a, b):
    return _dot(a, b, ((1,), (1,)))


def _tn(a, b):
    return _dot(a, b, ((0,), (0,)))


def _factor_tile(tile):
    count = tile.shape[0] // 8
    rows = [tile[8 * s : 8 * s + 8] for s in range(count)]
    lane = lax.broadcasted_iota(jnp.int32, (8, 128), 1)
    sub = lax.broadcasted_iota(jnp.int32, (8, 128), 0)

    def spread(x):
        return jnp.broadcast_to(x, (8, 128))

    def column(x, at):
        return jnp.take_along_axis(x, jnp.full((8, 128), at, jnp.int32), axis=1)

    upper, inverse = [], []
    own = [column(rows[0], k) for k in range(8)]
    for s in range(count):
        base = 8 * s
        stop = (s // GROUP + 1) * GROUP
        last = s + 1 == stop
        here = (lane >= base) & (lane < base + 8)
        ahead = [] if last else [column(rows[s], base + 8 + k) for k in range(8)]
        below = [] if last else [column(rows[s + 1], base + k) for k in range(8)]
        after = [] if last else [column(rows[s + 1], base + 8 + k) for k in range(8)]
        cols = {t: [column(rows[t], base + k) for k in range(8)] for t in range(s + 2, stop)}
        rows[s] = jnp.where(here, jnp.where(lane - base == sub, 1.0, 0.0), rows[s])
        for t in range(s + 1, stop):
            rows[t] = jnp.where(here, 0.0, rows[t])
        scales, pivots, pivot_rows = [], {}, []
        for j in range(8):
            scale = 1.0 / spread(own[j][j : j + 1, :])
            ratio = jnp.where(sub > j, own[j], 0.0) * scale
            for k in range(j + 1, 8):
                pivots[j, k] = spread(own[k][j : j + 1, :])
                own[k] = own[k] - ratio * pivots[j, k]
            pivot_row = spread(rows[s][j : j + 1, :])
            rows[s] = rows[s] - ratio * pivot_row
            scales.append(scale)
            pivot_rows.append(pivot_row)
            if not last:
                low = below[j] * scale
                for k in range(j + 1, 8):
                    below[k] = below[k] - low * pivots[j, k]
                for k in range(8):
                    pivot = spread(ahead[k][j : j + 1, :])
                    ahead[k] = ahead[k] - ratio * pivot
                    after[k] = after[k] - low * pivot
                rows[s + 1] = rows[s + 1] - low * pivot_row
        for t in range(s + 2, stop):
            other, row = cols[t], rows[t]
            for j in range(8):
                ratio = other[j] * scales[j]
                for k in range(j + 1, 8):
                    other[k] = other[k] - ratio * pivots[j, k]
                row = row - ratio * pivot_rows[j]
            rows[t] = row
        diag, square = own[0], own[0]
        for k in range(1, 8):
            diag = jnp.where(sub == k, own[k], diag)
            square = jnp.where(lane == base + k, own[k], square)
        root = lax.rsqrt(diag)
        square = jnp.where(sub <= lane - base, square, 0.0)
        upper.append(jnp.where(lane < base, 0.0, jnp.where(here, square, rows[s])) * root)
        inverse.append(jnp.where(lane < base + 8, rows[s], 0.0) * root)
        own = after
        if last and stop < count:
            low, high = 8 * (stop - GROUP), 8 * stop
            done = jnp.concatenate(upper[-GROUP:], 0)
            kept = jnp.where(lax.broadcasted_iota(jnp.int32, done.shape, 1) < high, jnp.concatenate(inverse[-GROUP:], 0), done)
            change = _tn(done, kept)
            for t in range(stop, count):
                inside = (lane >= low) & (lane < high)
                rows[t] = jnp.where(inside, 0.0, rows[t]) - change[8 * t : 8 * t + 8]
            own = [column(rows[stop], 8 * stop + k) for k in range(8)]
    return jnp.concatenate(upper, 0), jnp.concatenate(inverse, 0)


def _factor_block(block):
    h = NB // 2
    u11, v11 = _factor_tile(block[:h, :h])
    u12 = _nn(v11, block[:h, h:])
    u22, v22 = _factor_tile(block[h:, h:] - _tn(u12, u12))
    v21 = -_nn(v22, _tn(u12, v11))
    zero = jnp.zeros((h, h), F32)
    upper = jnp.concatenate([jnp.concatenate([u11, u12], 1), jnp.concatenate([zero, u22], 1)], 0)
    inverse = jnp.concatenate([jnp.concatenate([v11, zero], 1), jnp.concatenate([v21, v22], 1)], 0)
    return upper, inverse


EARLY = [(0, 0), (0, 1), (1, 1)]
LATE = [(1, 2), (2, 2), (2, 3), (3, 3), (3, 0), (0, 2), (1, 3)]


HALF = NB // 2


def _fetch(pairs, sems):
    copies = [pltpu.make_async_copy(x, y, sems.at[i]) for i, (x, y) in enumerate(pairs)]
    for copy in copies:
        copy.start()
    return copies


def _columns(half, rows):
    return pl.ds(half, rows, stride=2)


def _square(load):
    return jnp.concatenate([load(half).reshape(NB, HALF) for half in range(2)], 1)


def _paired(held, slot):
    def load(half):
        thin = held.shape[3] // 2
        return jnp.stack([held[core, :, slot, _columns(half, thin), :] for core in range(2)], 1)

    return _square(load)


def _early_kernel(own, other, upper, inverse, held, work, sems):
    core = lax.rem(lax.axis_index("col"), 2)
    count = len(EARLY)
    copies = _fetch([(x.at[:, pl.ds(0, count)], held.at[at]) for x, at in ((own, core), (other, 1 - core))], sems)
    for copy in copies:
        copy.wait()
    work[...] = _paired(held, 0)

    def panel(k, _):
        u, v = _factor_block(work[...])
        upper[k] = u
        inverse[k] = v

        @pl.when(k == 0)
        def _():
            u01 = _nn(inverse[0], _paired(held, 1))
            upper[2] = u01
            work[...] = _paired(held, 2) - _tn(u01, u01)

        return 0

    lax.fori_loop(0, 2, panel, 0)


def _late_kernel(own, other, upper, inverse, over, diag, inverse_out, held, u, v, sems):
    core = lax.rem(lax.axis_index("col"), 2)
    pairs = [(x.at[:, pl.ds(len(EARLY), len(LATE))], held.at[at]) for x, at in ((own, core), (other, 1 - core))]
    copies = _fetch([*pairs, (upper.at[2], u), (inverse, v)], sems)
    for copy in copies:
        copy.wait()

    def block(i, j):
        return _paired(held, LATE.index((i, j)))

    u02 = _nn(v[0], block(0, 2))
    u03 = _nt(v[0], block(3, 0))
    u12 = _nn(v[1], block(1, 2) - _tn(u[...], u02))
    u13 = _nn(v[1], block(1, 3) - _tn(u[...], u03))
    over[0], over[1], over[2], over[3] = u02, u03, u12, u13
    top, low = _factor_block(block(2, 2) - _tn(u02, u02) - _tn(u12, u12))
    u23 = _nn(low, block(2, 3) - _tn(u02, u03) - _tn(u12, u13))
    last = block(3, 3) - _tn(u03, u03) - _tn(u13, u13)
    diag[0], inverse_out[0], over[4] = top, low, u23
    diag[1], inverse_out[1] = _factor_block(last - _tn(u23, u23))


def _finish_kernel(
    kernel, left, top, early, inv01, over, diag, inv23,
    out, raw_left, raw_top, left_rows, top_cols, e, v, o, d, w, sems,
):
    row, col = lax.axis_index("row"), lax.axis_index("col")
    pairs = [(inv01, v.at[pl.ds(0, 2)]), (top.at[pl.ds(0, KP)], raw_top), (early, e), (left, raw_left), (over, o)]
    pairs += [(inv23, v.at[pl.ds(2, 2)]), (diag, d), (kernel, w)]
    copies = _fetch(pairs, sems)
    offs = {(0, 1): e.at[2], (2, 3): o.at[4]}
    offs.update({at: o.at[i] for i, at in enumerate([(0, 2), (0, 3), (1, 2), (1, 3)])})
    thin = raw_left.shape[3] // 2

    def step_top(k):
        head = _square(lambda half: raw_top[k, _columns(half, NB), :])
        for j in range(k):
            head = head - _tn(offs[j, k][...], top_cols[j])
        top_cols[k] = _nn(v[k], head)

    def step_left(k):
        parts = [_square(lambda half: raw_left[:, k, l, _columns(half, thin), :]) for l in range(2)]
        for j in range(k):
            parts = [parts[l] - _nn(left_rows[j, pl.ds(NB * l, NB)], offs[j, k][...]) for l in range(2)]
        for l in range(2):
            left_rows[k, pl.ds(NB * l, NB)] = _nt(parts[l], v[k])

    for copy in copies[:3]:
        copy.wait()
    step_top(0)
    step_top(1)
    for copy in copies[3:]:
        copy.wait()
    step_left(0)
    step_left(1)
    for k in (2, 3):
        step_top(k)
        step_left(k)

    def store(l, block):
        for half in range(2):
            out[l, _columns(half, NB), :] = block[:, half * HALF : (half + 1) * HALF]

    @pl.when(col >= KP)
    def _():
        total = jnp.concatenate([_square(lambda half: w[l, _columns(half, NB), :]) for l in range(2)], 0)
        for k in range(KP):
            total = total - _nn(left_rows[k], top_cols[k])
        store(0, jnp.where(row < KP, 0.0, total[:NB]))
        store(1, total[NB:])

    @pl.when(col < KP)
    def _():
        block = left_rows[col]
        store(0, jnp.where(row < col, 0.0, block[:NB]))
        store(1, block[NB:])

    for k in range(KP):

        @pl.when((row == k) & (col == k))
        def _():
            store(0, (e if k < 2 else d)[k % 2].T)


VMEM = pl.BlockSpec(memory_space=pltpu.VMEM)
ANYWHERE = pl.BlockSpec(memory_space=pl.ANY)


def _tiles(*lead):
    return jax.ShapeDtypeStruct((*lead, NB, NB), F32)


def _scratch(*lead):
    return pltpu.VMEM((*lead, NB, NB), F32)


def _call(kernel, name, cost, copies, scratch, out_shape, operands):
    return pl.pallas_call(
        kernel,
        out_shape=out_shape,
        in_specs=[ANYWHERE] * len(operands),
        out_specs=jax.tree.map(lambda _: VMEM, out_shape),
        scratch_shapes=[*scratch, pltpu.SemaphoreType.DMA((copies,))],
        compiler_params=pltpu.CompilerParams(vmem_limit_bytes=60 * MIB),
        cost_estimate=pl.CostEstimate(flops=cost * 10**9, bytes_accessed=4_000_000, transcendentals=0),
        name=name,
    )(*operands)


def _early(own, other):
    held = pltpu.VMEM((2, own.shape[0], len(EARLY), *own.shape[2:]), F32)
    return _call(_early_kernel, "early", 12, 2, [held, _scratch()], (_tiles(3), _tiles(2)), (own, other))


def _late(own, other, upper, inverse):
    held = pltpu.VMEM((2, own.shape[0], len(LATE), *own.shape[2:]), F32)
    return _call(
        _late_kernel,
        "late",
        16,
        4,
        [held, _scratch(), _scratch(2)],
        (_tiles(5), _tiles(2), _tiles(2)),
        (own, other, upper, inverse),
    )


def _finish(blocks, left, top, early, inv01, over, diag, inv23):
    scratch = [
        pltpu.VMEM(left.shape, F32),
        pltpu.VMEM((KP, *top.shape[1:]), F32),
        pltpu.VMEM((KP, 2 * NB, NB), F32),
        _scratch(KP),
        _scratch(3),
        _scratch(KP),
        _scratch(5),
        _scratch(2),
        pltpu.VMEM(blocks.shape, F32),
    ]
    return _call(
        _finish_kernel,
        "finish",
        10,
        8,
        scratch,
        jax.ShapeDtypeStruct(blocks.shape, F32),
        (blocks, left, top, early, inv01, over, diag, inv23),
    )


def on_device(kernel):
    rows_axis, cols_axis = lax.axis_size("row"), lax.axis_size("col")
    row_index, col_index = lax.axis_index("row"), lax.axis_index("col")
    blocks = kernel.reshape(2, 2 * NB, HALF)
    piece = (2 * NB // cols_axis, HALF)
    cores = [list(range(core, cols_axis, 2)) for core in range(2)]
    quads = [list(range(r, r + KP)) for r in range(0, rows_axis, KP)]

    def copies(x, count):
        return jnp.broadcast_to(x[None], (count, *x.shape))

    def spread(whole, axis, groups=None):
        return lax.all_to_all(whole, axis, 0, 0, axis_index_groups=groups)

    def swap(x):
        return lax.ppermute(x, "col", [(c, c ^ 1) for c in range(cols_axis)])

    cut = blocks.reshape(2, cols_axis, *piece).swapaxes(0, 1)
    scattered = lax.all_to_all(cut, "col", 0, 0)[:KP]

    lead, scattered = lax.optimization_barrier((blocks[0], scattered))
    top = lax.all_gather(lead, "row")

    first = scattered[:, 0]
    mine = jnp.stack([lax.dynamic_index_in_dim(first, lax.rem(row_index + o, KP), 0, keepdims=False) for o in range(3)])
    far = [lax.ppermute(mine, "row", [(r, r + d) for r in range(KP)]) for d in range(KP, rows_axis, KP)]
    mine = jnp.where(row_index < KP, mine, sum(far))
    mine, left = lax.optimization_barrier((mine, copies(scattered, cols_axis)))
    corner = spread(copies(mine, KP), "row", quads)

    order = [corner[r, (c - r) % KP] for r, c in EARLY + LATE]
    own = spread(copies(jnp.stack(order), cols_axis // 2), "col", cores)
    other = swap(own)
    left, _ = lax.optimization_barrier((left, own))
    left = spread(left, "col")

    early, inv01 = _early(own, other)
    over, diag, inv23 = _late(own, other, early, inv01)
    out = _finish(blocks, left, top, early, inv01, over, diag, inv23)
    return out.reshape(kernel.shape)


def solution(mesh):
    spec = P(None, "row", None, "col")
    return jax.shard_map(
        on_device, mesh=mesh, in_specs=(spec,), out_specs=spec, check_vma=False
    )
```
